32 devices in a mesh: grp: 2 (over x), chan: 16 (over z, y, core).
Axes of the slice: x: 2, y: 2, z: 4, core: 2. Of those that a mesh axis runs over, the one named last changes fastest.
Arguments:
- voltages_real: int32 [256, 32, 1024], P('chan', 'grp'), parts along dimension 1, may hold values from -127 to 127, as said below
- voltages_imag: int32 [256, 32, 1024], P('chan', 'grp'), parts along dimension 1, may hold values from -127 to 127, as said below
- model: bfloat16 [2, 128, 4608], replicated, may hold values from -10 to 10
- gains: float32 [2, 2048], P(None, 'grp'), parts along dimension 1, may hold values from -2.5 to 2.5
- bandpass: float32 [32], P(('grp', 'chan')), parts along dimension 0, may hold values from 0.3 to 3.3
Outputs:
- residual: float32 [32, 2, 128, 4608], P(('grp', 'chan')), parts along dimension 0
- new_gains: float32 [2, 2048], P(None, ('grp', 'chan')), parts along dimension 1
The draws below stay inside these ranges and needn't reach their ends.
There are 2 independent parts, one for each index of `grp`. The reference program is written for one: setup_inputs(seed, part) draws one part's arguments, and reference() takes and returns one part's arrays. A program takes and returns all parts, laid end to end along the dimension named above; an argument that names none is the same for every part. Nothing has to cross between parts.
Inputs may be any that keep to these rules, and one draw needn't show every extreme that they name: `voltages_real`: quantized voltage components, saturated symmetrically at -127 and 127. `voltages_imag`: quantized voltage components, saturated symmetrically at -127 and 127.
All inputs are finite; a program needn't handle non-finite values.
Results may differ from the reference program's by a relative error of at most 0.0003.
Values may be sent and summed in bfloat16 or wider, within the bound.
A program may use at most 128 MiB of HBM per device.

```python
import math
import jax
import jax.numpy as jnp
from jax import lax

INPUTS = 1024
TILE = 128
SAMPLES = 256
CHANNELS = 16


def sky_parts(key):
    keys = jax.random.split(key, 4)
    weight_real = jax.random.randint(keys[0], (CHANNELS, INPUTS, 2), -4, 5)
    weight_imag = jax.random.randint(keys[1], (CHANNELS, INPUTS, 2), -4, 5)
    signal_real = jax.random.randint(keys[2], (SAMPLES, CHANNELS, 2), -8, 9)
    signal_imag = jax.random.randint(keys[3], (SAMPLES, CHANNELS, 2), -8, 9)
    return (weight_real, weight_imag, signal_real, signal_imag)


def sky_sum(signal_first, weight_first, signal_second, weight_second, sign_value):
    total = jnp.zeros((SAMPLES, CHANNELS, INPUTS), jnp.int32)
    for source in range(2):
        total = total + signal_first[:, :, None, source] * weight_first[None, :, :, source]
        total = total + sign_value * signal_second[:, :, None, source] * weight_second[None, :, :, source]
    return total


def draw_voltages_real(key, part):
    weight_real, weight_imag, signal_real, signal_imag = sky_parts(key)
    key = jax.random.fold_in(key, 11)
    noise = jax.random.randint(key, (SAMPLES, CHANNELS, INPUTS), -48, 49)
    sky = sky_sum(signal_real, weight_real, signal_imag, weight_imag, -1)
    return jnp.clip(2 * sky + noise, -127, 127).astype(jnp.int32)


def draw_voltages_imag(key, part):
    weight_real, weight_imag, signal_real, signal_imag = sky_parts(key)
    key = jax.random.fold_in(key, 13)
    noise = jax.random.randint(key, (SAMPLES, CHANNELS, INPUTS), -48, 49)
    sky = sky_sum(signal_real, weight_imag, signal_imag, weight_real, 1)
    return jnp.clip(2 * sky + noise, -127, 127).astype(jnp.int32)


def draw_model(key, part):
    key = jax.random.fold_in(key, 21)
    first_key, second_key = jax.random.split(key)
    values = jnp.clip(jax.random.normal(first_key, (2, INPUTS, INPUTS), jnp.float32), -3.0, 3.0)
    scales = jnp.exp(jax.random.uniform(second_key, (INPUTS,), jnp.float32, -0.6, 0.6))
    full = values * scales[None, :, None] * scales[None, None, :]
    block_count = INPUTS // TILE
    packed = jnp.concatenate([full[:, stripe * TILE:(stripe + 1) * TILE, :(stripe + 1) * TILE] for stripe in range(block_count)], axis=-1)
    return packed.astype(jnp.bfloat16)


def draw_bandpass(key, part):
    key = jax.random.fold_in(key, 31)
    spread = 0.35
    jitter = jax.random.uniform(key, (CHANNELS,), jnp.float32, -spread, spread)
    ramp = jnp.arange(CHANNELS, dtype=jnp.float32) / (CHANNELS - 1)
    return (0.6 * jnp.exp(ramp * math.log(3.0) + jitter)).astype(jnp.float32)


def normal_values(stream_key, extent, width, reach, held_as=jnp.bfloat16):
    return jnp.clip(width * jax.random.normal(stream_key, extent, jnp.float32), -reach, reach).astype(held_as)


def setup_inputs(seed: int = 0, part: int = 0) -> dict:
    key_list = jax.random.split(jax.random.key(seed), 6)
    part_splits = jax.random.split(jax.random.fold_in(key_list[5], part), 6)
    voltages_real = draw_voltages_real(jax.random.fold_in(jax.random.fold_in(key_list[5], part), 71), part)
    voltages_imag = draw_voltages_imag(jax.random.fold_in(jax.random.fold_in(key_list[5], part), 71), part)
    model = draw_model(jax.random.fold_in(key_list[5], 71), part)
    gains = normal_values(part_splits[3], (2, INPUTS), 0.7, 2.5, jnp.float32)
    bandpass = draw_bandpass(jax.random.fold_in(jax.random.fold_in(key_list[5], part), 71), part)
    return dict(voltages_real=voltages_real, voltages_imag=voltages_imag, model=model, gains=gains, bandpass=bandpass)


def pack_rows(matrix, tile_width, block_count):
    return jnp.concatenate([matrix[..., stripe * tile_width:(stripe + 1) * tile_width, :(stripe + 1) * tile_width] for stripe in range(block_count)], axis=-1)


def strip_terms(q_real, q_imag, gain_real, gain_imag, stripe, tile_width, input_count):
    start = stripe * tile_width
    span = (stripe + 1) * tile_width
    col_real = gain_real[:span]
    col_imag = gain_imag[:span]
    own_real = gain_real[start:span]
    own_imag = gain_imag[start:span]
    f32 = jnp.float32
    row_re = jnp.dot(q_real, col_real, preferred_element_type=f32) - jnp.dot(q_imag, col_imag, preferred_element_type=f32)
    row_im = jnp.dot(q_real, col_imag, preferred_element_type=f32) + jnp.dot(q_imag, col_real, preferred_element_type=f32)
    col_re = jnp.dot(own_real, q_real, preferred_element_type=f32) + jnp.dot(own_imag, q_imag, preferred_element_type=f32)
    col_im = jnp.dot(own_imag, q_real, preferred_element_type=f32) - jnp.dot(own_real, q_imag, preferred_element_type=f32)
    total_real = jnp.zeros((input_count,), jnp.float32).at[:span].add(col_re).at[start:span].add(row_re)
    total_imag = jnp.zeros((input_count,), jnp.float32).at[:span].add(col_im).at[start:span].add(row_im)
    return jnp.stack([total_real, total_imag])


def reference(voltages_real, voltages_imag, model, gains, bandpass):
    tile_width = TILE
    block_count = INPUTS // TILE
    scale_factor = 1.0 / (4096.0 * SAMPLES)
    gain_real = gains[0]
    gain_imag = gains[1]
    short_real = gain_real.astype(jnp.bfloat16)
    short_imag = gain_imag.astype(jnp.bfloat16)
    model_real = model[0].astype(jnp.float32)
    model_imag = model[1].astype(jnp.float32)
    outer_real = pack_rows(gain_real[:, None] * gain_real[None, :] + gain_imag[:, None] * gain_imag[None, :], tile_width, block_count)
    outer_imag = pack_rows(gain_imag[:, None] * gain_real[None, :] - gain_real[:, None] * gain_imag[None, :], tile_width, block_count)
    pred_real = outer_real * model_real - outer_imag * model_imag
    pred_imag = outer_real * model_imag + outer_imag * model_real

    def one_channel(channel_index):
        volt_real = lax.dynamic_index_in_dim(voltages_real, channel_index, 1, keepdims=False).astype(jnp.bfloat16)
        volt_imag = lax.dynamic_index_in_dim(voltages_imag, channel_index, 1, keepdims=False).astype(jnp.bfloat16)
        gram_real = jnp.dot(volt_real.T, volt_real, preferred_element_type=jnp.float32) + jnp.dot(volt_imag.T, volt_imag, preferred_element_type=jnp.float32)
        gram_imag = jnp.dot(volt_imag.T, volt_real, preferred_element_type=jnp.float32) - jnp.dot(volt_real.T, volt_imag, preferred_element_type=jnp.float32)
        weight = lax.dynamic_index_in_dim(bandpass, channel_index, 0, keepdims=False)
        res_real = pack_rows(gram_real, tile_width, block_count) * scale_factor - weight * pred_real
        res_imag = pack_rows(gram_imag, tile_width, block_count) * scale_factor - weight * pred_imag
        q_real = (weight * (res_real * model_real + res_imag * model_imag)).astype(jnp.bfloat16)
        q_imag = (weight * (res_imag * model_real - res_real * model_imag)).astype(jnp.bfloat16)
        terms = jnp.zeros((2, INPUTS), jnp.float32)
        for stripe in range(block_count):
            offset = tile_width * stripe * (stripe + 1) // 2
            span = (stripe + 1) * tile_width
            terms = terms + strip_terms(q_real[:, offset:offset + span], q_imag[:, offset:offset + span], short_real, short_imag, stripe, tile_width, INPUTS)
        return jnp.stack([res_real, res_imag]), terms

    residual, terms = lax.map(one_channel, jnp.arange(CHANNELS, dtype=jnp.int32))
    grad = -jnp.sum(terms, axis=0)
    power_gain = gain_real * gain_real + gain_imag * gain_imag
    geom = jnp.zeros((INPUTS,), jnp.float32)
    for stripe in range(block_count):
        offset = tile_width * stripe * (stripe + 1) // 2
        start = stripe * tile_width
        span = (stripe + 1) * tile_width
        weight_sq = model_real[:, offset:offset + span] ** 2 + model_imag[:, offset:offset + span] ** 2
        geom = geom.at[start:span].add(jnp.sum(weight_sq * power_gain[None, :span], axis=1))
        geom = geom.at[:span].add(jnp.sum(power_gain[start:span][:, None] * weight_sq, axis=0))
    power = jnp.sum(bandpass * bandpass)
    new_gains = gains - 0.5 * grad / (power * geom)[None, :]
    return residual, new_gains
```

```python
import functools

import jax
import jax.numpy as jnp
from jax import lax
from jax.experimental import pallas as pl
from jax.experimental.pallas import tpu as pltpu
from jax.sharding import PartitionSpec as P

F32 = jnp.float32
BF16 = jnp.bfloat16
LANES = 128


def partner_of(me, step, count):
    total = 0
    bit = 1
    while bit < count:
        total = total + lax.rem(lax.div(me, bit) + lax.div(step, bit), 2) * bit
        bit *= 2
    return total


def lane_block(index):
    return pl.ds(pl.multiple_of(index * LANES, LANES), LANES)


def fold_rows(block):
    return jnp.sum(block.reshape(block.shape[0] // 8, 8, block.shape[1]), axis=0)


def column_sum(block):
    return jnp.sum(block, axis=0, keepdims=True)


def kernel(
    count,
    scale,
    vr_hbm,
    vi_hbm,
    model_hbm,
    gain_ref,
    band_ref,
    res_ref,
    new_ref,
    ints,
    outgoing,
    volts,
    swapped,
    model,
    gain_rows,
    row_acc,
    col_acc,
    geom_col,
    geom_all,
    terms,
    incoming,
    load_sem,
    model_sem,
    send_sem,
    recv_sem,
    term_send,
    term_recv,
):
    me = lax.axis_index("chan")
    inputs = gain_ref.shape[1]
    blocks = inputs // LANES
    samples = ints.shape[2] // count
    share = new_ref.shape[1]

    loads = []
    for which, source in enumerate((vr_hbm, vi_hbm)):
        for lane in range(blocks):
            load = pltpu.make_async_copy(
                source.at[:, lane * LANES : (lane + 1) * LANES],
                ints.at[which, lane],
                load_sem.at[which, lane],
            )
            load.start()
            loads.append(load)
    load_model = pltpu.make_async_copy(model_hbm, model, model_sem)

    barrier = pltpu.get_barrier_semaphore()

    @pl.loop(1, count)
    def _(step):
        pl.semaphore_signal(
            barrier,
            inc=1,
            device_id={"chan": partner_of(me, step, count)},
            device_id_type=pl.DeviceIdType.MESH,
        )

    for load in loads:
        load.wait()
    load_model.start()
    pl.semaphore_wait(barrier, count - 1)

    def volt_copy(step):
        return pltpu.make_async_remote_copy(
            src_ref=outgoing.at[step],
            dst_ref=volts.at[step],
            send_sem=send_sem.at[step],
            recv_sem=recv_sem.at[step],
            device_id={"chan": partner_of(me, step, count)},
            device_id_type=pl.DeviceIdType.MESH,
        )

    def short_rows(which, channel, lane):
        rows = ints[which, lane, pl.ds(channel, samples, stride=count), :]
        return rows.astype(F32).astype(BF16)

    @pl.loop(0, count - 1)
    def _(turn):
        step = count - 1 - turn
        channel = partner_of(me, step, count)
        for lane in range(blocks):
            cols = slice(lane * LANES, (lane + 1) * LANES)
            outgoing[step, 0:samples, cols] = short_rows(0, channel, lane)
            outgoing[step, samples : 2 * samples, cols] = short_rows(1, channel, lane)
        volt_copy(step).start()

    for lane in range(blocks):
        cols = slice(lane * LANES, (lane + 1) * LANES)
        volts[0, 0:samples, cols] = short_rows(0, me, lane)
        volts[0, samples : 2 * samples, cols] = short_rows(1, me, lane)

    band = band_ref[0]

    @pl.loop(0, blocks)
    def _(p):
        for part in range(2):
            line = gain_ref[part : part + 1, lane_block(p)]
            gain_rows[part, lane_block(p), :] = jnp.broadcast_to(line, (LANES, LANES)).T
        geom_col[p] = jnp.zeros((8, LANES), F32)
        col_acc[p] = jnp.zeros((2, 8, LANES), F32)

    load_model.wait()

    @pl.loop(0, blocks)
    def _(p):
        row_acc[0] = jnp.zeros((LANES, LANES), F32)
        rows = lane_block(p)

        @pl.loop(0, p + 1)
        def _(j):
            place = lane_block(lax.div(p * (p + 1), 2) + j)
            model_real = model[0, :, place].astype(F32)
            model_imag = model[1, :, place].astype(F32)
            row_real = gain_rows[0, rows, :]
            row_imag = gain_rows[1, rows, :]
            col_real = gain_ref[0:1, lane_block(j)]
            col_imag = gain_ref[1:2, lane_block(j)]
            outer_real = row_real * col_real + row_imag * col_imag
            outer_imag = row_imag * col_real - row_real * col_imag
            res_ref[0, 0, :, place] = -band * (outer_real * model_real - outer_imag * model_imag)
            res_ref[0, 1, :, place] = -band * (outer_real * model_imag + outer_imag * model_real)
            weight_sq = model_real * model_real + model_imag * model_imag
            row_acc[0] += weight_sq * (col_real * col_real + col_imag * col_imag)
            geom_col[j] += fold_rows((row_real * row_real + row_imag * row_imag) * weight_sq)

        geom_all[p] = column_sum(row_acc[0].T)

    def gather_products(first, last):
        @pl.loop(max(first, 1), last)
        def _(step):
            volt_copy(step).wait_recv()

        @pl.loop(first, last)
        def _(step):
            swapped[step, 0:samples, :] = -volts[step, samples : 2 * samples, :]
            swapped[step, samples : 2 * samples, :] = volts[step, 0:samples, :]

        depth = (last - first) * 2 * samples
        wide = 2 * LANES
        for pair in range(blocks // 2):
            left = volts[first:last, :, pair * wide : (pair + 1) * wide].reshape(depth, wide)
            for tile in range(pair + 1):
                for part, source in ((0, volts), (1, swapped)):
                    right = source[first:last, :, tile * wide : (tile + 1) * wide].reshape(depth, wide)
                    product = scale * lax.dot_general(
                        left, right, (((0,), (0,)), ((), ())), preferred_element_type=F32
                    )
                    for half in range(2):
                        stripe = 2 * pair + half
                        offset = stripe * (stripe + 1) // 2 * LANES + tile * wide
                        width = min(wide, (stripe + 1) * LANES - tile * wide)
                        res_ref[0, part, :, offset : offset + width] += product[
                            half * LANES : (half + 1) * LANES, :width
                        ]

    gather_products(0, count // 2)
    gather_products(count // 2, count)

    @pl.loop(0, blocks)
    def _(p):
        row_acc[...] = jnp.zeros((2, LANES, LANES), F32)
        rows = lane_block(p)

        @pl.loop(0, p + 1)
        def _(j):
            place = lane_block(lax.div(p * (p + 1), 2) + j)
            model_real = model[0, :, place].astype(F32)
            model_imag = model[1, :, place].astype(F32)
            res_real = res_ref[0, 0, :, place]
            res_imag = res_ref[0, 1, :, place]
            q_real = (band * (res_real * model_real + res_imag * model_imag)).astype(BF16).astype(F32)
            q_imag = (band * (res_imag * model_real - res_real * model_imag)).astype(BF16).astype(F32)
            col_real = gain_ref[0:1, lane_block(j)].astype(BF16).astype(F32)
            col_imag = gain_ref[1:2, lane_block(j)].astype(BF16).astype(F32)
            row_real = gain_rows[0, rows, :].astype(BF16).astype(F32)
            row_imag = gain_rows[1, rows, :].astype(BF16).astype(F32)
            row_acc[0] += q_real * col_real - q_imag * col_imag
            row_acc[1] += q_real * col_imag + q_imag * col_real
            col_acc[j, 0] += fold_rows(row_real * q_real + row_imag * q_imag)
            col_acc[j, 1] += fold_rows(row_imag * q_real - row_real * q_imag)

        terms[p, 0:1] = column_sum(row_acc[0].T)
        terms[p, 1:2] = column_sum(row_acc[1].T)
        terms[p, 2:3] = jnp.full((1, LANES), band * band, F32)
        terms[p, 3:8] = jnp.zeros((5, LANES), F32)

    @pl.loop(0, blocks)
    def _(p):
        terms[p, 0:1] += column_sum(col_acc[p, 0])
        terms[p, 1:2] += column_sum(col_acc[p, 1])

    def term_copy(step):
        target = partner_of(me, step, count)
        return pltpu.make_async_remote_copy(
            src_ref=terms.at[lax.div(target * share, LANES)],
            dst_ref=incoming.at[step],
            send_sem=term_send.at[step],
            recv_sem=term_recv.at[step],
            device_id={"chan": target},
            device_id_type=pl.DeviceIdType.MESH,
        )

    @pl.loop(0, count - 1)
    def _(turn):
        term_copy(count - 1 - turn).start()

    mine = lax.div(me * share, LANES)
    incoming[0] = terms[mine]

    @pl.loop(1, count)
    def _(step):
        volt_copy(step).wait_send()
        term_copy(step).wait()

    total = jnp.sum(incoming[...], axis=0)
    geom = geom_all[mine] + column_sum(geom_col[mine])
    updated = gain_ref[:, lane_block(mine)] + 0.5 * total[0:2] / (total[2:3] * geom)
    lane_group = lax.rem(me, LANES // share)
    picked = updated[:, 0:share]
    for group in range(1, LANES // share):
        picked = jnp.where(lane_group == group, updated[:, group * share : (group + 1) * share], picked)
    new_ref[...] = picked


def shards(voltages_real, voltages_imag, model, gains, bandpass):
    count = lax.axis_size("chan")
    samples, channels, inputs = voltages_real.shape
    scale = 1.0 / (4096.0 * samples * count)
    blocks = inputs // LANES
    share = inputs // count
    anywhere = pl.BlockSpec(memory_space=pl.ANY)
    in_vmem = pl.BlockSpec(memory_space=pltpu.VMEM)
    return pl.pallas_call(
        functools.partial(kernel, count, scale),
        out_shape=(
            jax.ShapeDtypeStruct((1,) + model.shape, F32),
            jax.ShapeDtypeStruct((2, share), F32),
        ),
        in_specs=[anywhere, anywhere, anywhere, in_vmem, pl.BlockSpec(memory_space=pltpu.SMEM)],
        out_specs=(in_vmem, in_vmem),
        scratch_shapes=[
            pltpu.VMEM((2, blocks, samples * channels, LANES), jnp.int32),
            pltpu.VMEM((count, 2 * samples, inputs), BF16),
            pltpu.VMEM((count, 2 * samples, inputs), BF16),
            pltpu.VMEM((count, 2 * samples, inputs), BF16),
            pltpu.VMEM(model.shape, BF16),
            pltpu.VMEM((2, inputs, LANES), F32),
            pltpu.VMEM((2, LANES, LANES), F32),
            pltpu.VMEM((blocks, 2, 8, LANES), F32),
            pltpu.VMEM((blocks, 8, LANES), F32),
            pltpu.VMEM((blocks, 1, LANES), F32),
            pltpu.VMEM((blocks, 8, LANES), F32),
            pltpu.VMEM((count, 8, LANES), F32),
            pltpu.SemaphoreType.DMA((2, blocks)),
            pltpu.SemaphoreType.DMA,
            pltpu.SemaphoreType.DMA((count,)),
            pltpu.SemaphoreType.DMA((count,)),
            pltpu.SemaphoreType.DMA((count,)),
            pltpu.SemaphoreType.DMA((count,)),
        ],
        compiler_params=pltpu.CompilerParams(
            collective_id=0, has_side_effects=True, vmem_limit_bytes=50 * 1024 * 1024
        ),
        cost_estimate=pl.CostEstimate(
            flops=4 * samples * count * inputs * inputs, bytes_accessed=10 * 1024 * 1024, transcendentals=0
        ),
    )(
        voltages_real.reshape(samples * channels, inputs),
        voltages_imag.reshape(samples * channels, inputs),
        model,
        gains,
        bandpass,
    )


def solution(mesh):
    in_specs = (
        P("chan", "grp", None),
        P("chan", "grp", None),
        P(),
        P(None, "grp"),
        P(("grp", "chan")),
    )
    out_specs = (P(("grp", "chan"), None, None, None), P(None, ("grp", "chan")))
    return jax.shard_map(shards, mesh=mesh, in_specs=in_specs, out_specs=out_specs, check_vma=False)
```

```python
import functools

import jax
import jax.numpy as jnp
from jax import lax
from jax.experimental import pallas as pl
from jax.experimental.pallas import tpu as pltpu
from jax.sharding import PartitionSpec as P

F32 = jnp.float32
BF16 = jnp.bfloat16
LANES = 128


def partner_of(me, step, count):
    total = 0
    bit = 1
    while bit < count:
        total = total + lax.rem(lax.div(me, bit) + lax.div(step, bit), 2) * bit
        bit *= 2
    return total


def lane_block(index):
    return pl.ds(pl.multiple_of(index * LANES, LANES), LANES)


def fold_rows(block):
    return jnp.sum(block.reshape(block.shape[0] // 8, 8, block.shape[1]), axis=0)


def column_sum(block):
    return jnp.sum(block, axis=0, keepdims=True)


def kernel(
    count,
    scale,
    vr_hbm,
    vi_hbm,
    model_hbm,
    gain_hbm,
    band_ref,
    res_ref,
    new_ref,
    ints,
    outgoing,
    volts,
    swapped,
    model,
    gain_ref,
    gain_rows,
    row_acc,
    col_acc,
    geom_col,
    geom_all,
    terms,
    incoming,
    load_sem,
    model_sem,
    gain_sem,
    send_sem,
    recv_sem,
    term_send,
    term_recv,
):
    me = lax.axis_index("chan")
    inputs = gain_ref.shape[1]
    blocks = inputs // LANES
    samples = ints.shape[2] // count
    share = new_ref.shape[1]

    loads = []
    for which, source in enumerate((vr_hbm, vi_hbm)):
        for lane in range(blocks):
            load = pltpu.make_async_copy(
                source.at[:, lane * LANES : (lane + 1) * LANES],
                ints.at[which, lane],
                load_sem.at[which, lane],
            )
            load.start()
            loads.append(load)
    load_gains = pltpu.make_async_copy(gain_hbm, gain_ref, gain_sem)
    load_model = pltpu.make_async_copy(model_hbm, model, model_sem)

    barrier = pltpu.get_barrier_semaphore()

    @pl.loop(1, count)
    def _(step):
        pl.semaphore_signal(
            barrier,
            inc=1,
            device_id={"chan": partner_of(me, step, count)},
            device_id_type=pl.DeviceIdType.MESH,
        )

    for load in loads:
        load.wait()
    load_gains.start()
    load_model.start()
    pl.semaphore_wait(barrier, count - 1)

    def volt_copy(step):
        return pltpu.make_async_remote_copy(
            src_ref=outgoing.at[step],
            dst_ref=volts.at[step],
            send_sem=send_sem.at[step],
            recv_sem=recv_sem.at[step],
            device_id={"chan": partner_of(me, step, count)},
            device_id_type=pl.DeviceIdType.MESH,
        )

    def short_rows(which, channel, lane):
        rows = ints[which, lane, pl.ds(channel, samples, stride=count), :]
        return rows.astype(F32).astype(BF16)

    @pl.loop(0, count - 1)
    def _(turn):
        step = count - 1 - turn
        channel = partner_of(me, step, count)
        for lane in range(blocks):
            cols = slice(lane * LANES, (lane + 1) * LANES)
            outgoing[step, 0:samples, cols] = short_rows(0, channel, lane)
            outgoing[step, samples : 2 * samples, cols] = short_rows(1, channel, lane)
        volt_copy(step).start()

    for lane in range(blocks):
        cols = slice(lane * LANES, (lane + 1) * LANES)
        volts[0, 0:samples, cols] = short_rows(0, me, lane)
        volts[0, samples : 2 * samples, cols] = short_rows(1, me, lane)

    band = band_ref[0]
    load_gains.wait()

    @pl.loop(0, blocks)
    def _(p):
        for part in range(2):
            line = gain_ref[part : part + 1, lane_block(p)]
            gain_rows[part, lane_block(p), :] = jnp.broadcast_to(line, (LANES, LANES)).T
        geom_col[p] = jnp.zeros((8, LANES), F32)
        col_acc[p] = jnp.zeros((2, 8, LANES), F32)

    load_model.wait()

    @pl.loop(0, blocks)
    def _(p):
        row_acc[0] = jnp.zeros((LANES, LANES), F32)
        rows = lane_block(p)

        @pl.loop(0, p + 1)
        def _(j):
            place = lane_block(lax.div(p * (p + 1), 2) + j)
            model_real = model[0, :, place].astype(F32)
            model_imag = model[1, :, place].astype(F32)
            row_real = gain_rows[0, rows, :]
            row_imag = gain_rows[1, rows, :]
            col_real = gain_ref[0:1, lane_block(j)]
            col_imag = gain_ref[1:2, lane_block(j)]
            outer_real = row_real * col_real + row_imag * col_imag
            outer_imag = row_imag * col_real - row_real * col_imag
            res_ref[0, 0, :, place] = -band * (outer_real * model_real - outer_imag * model_imag)
            res_ref[0, 1, :, place] = -band * (outer_real * model_imag + outer_imag * model_real)
            weight_sq = model_real * model_real + model_imag * model_imag
            row_acc[0] += weight_sq * (col_real * col_real + col_imag * col_imag)
            geom_col[j] += fold_rows((row_real * row_real + row_imag * row_imag) * weight_sq)

        geom_all[p] = column_sum(row_acc[0].T)

    def gather_products(first, last):
        @pl.loop(max(first, 1), last)
        def _(step):
            volt_copy(step).wait_recv()

        @pl.loop(first, last)
        def _(step):
            swapped[step, 0:samples, :] = -volts[step, samples : 2 * samples, :]
            swapped[step, samples : 2 * samples, :] = volts[step, 0:samples, :]

        depth = (last - first) * 2 * samples
        wide = 2 * LANES
        for pair in range(blocks // 2):
            left = volts[first:last, :, pair * wide : (pair + 1) * wide].reshape(depth, wide)
            for tile in range(pair + 1):
                for part, source in ((0, volts), (1, swapped)):
                    right = source[first:last, :, tile * wide : (tile + 1) * wide].reshape(depth, wide)
                    product = scale * lax.dot_general(
                        left, right, (((0,), (0,)), ((), ())), preferred_element_type=F32
                    )
                    for half in range(2):
                        stripe = 2 * pair + half
                        offset = stripe * (stripe + 1) // 2 * LANES + tile * wide
                        width = min(wide, (stripe + 1) * LANES - tile * wide)
                        res_ref[0, part, :, offset : offset + width] += product[
                            half * LANES : (half + 1) * LANES, :width
                        ]

    gather_products(0, count // 2)
    gather_products(count // 2, count)

    @pl.loop(0, blocks)
    def _(p):
        row_acc[...] = jnp.zeros((2, LANES, LANES), F32)
        rows = lane_block(p)

        @pl.loop(0, p + 1)
        def _(j):
            place = lane_block(lax.div(p * (p + 1), 2) + j)
            model_real = model[0, :, place].astype(F32)
            model_imag = model[1, :, place].astype(F32)
            res_real = res_ref[0, 0, :, place]
            res_imag = res_ref[0, 1, :, place]
            q_real = (band * (res_real * model_real + res_imag * model_imag)).astype(BF16).astype(F32)
            q_imag = (band * (res_imag * model_real - res_real * model_imag)).astype(BF16).astype(F32)
            col_real = gain_ref[0:1, lane_block(j)].astype(BF16).astype(F32)
            col_imag = gain_ref[1:2, lane_block(j)].astype(BF16).astype(F32)
            row_real = gain_rows[0, rows, :].astype(BF16).astype(F32)
            row_imag = gain_rows[1, rows, :].astype(BF16).astype(F32)
            row_acc[0] += q_real * col_real - q_imag * col_imag
            row_acc[1] += q_real * col_imag + q_imag * col_real
            col_acc[j, 0] += fold_rows(row_real * q_real + row_imag * q_imag)
            col_acc[j, 1] += fold_rows(row_imag * q_real - row_real * q_imag)

        terms[p, 0:1] = column_sum(row_acc[0].T)
        terms[p, 1:2] = column_sum(row_acc[1].T)
        terms[p, 2:3] = jnp.full((1, LANES), band * band, F32)
        terms[p, 3:8] = jnp.zeros((5, LANES), F32)

    @pl.loop(0, blocks)
    def _(p):
        terms[p, 0:1] += column_sum(col_acc[p, 0])
        terms[p, 1:2] += column_sum(col_acc[p, 1])

    def term_copy(step):
        target = partner_of(me, step, count)
        return pltpu.make_async_remote_copy(
            src_ref=terms.at[lax.div(target * share, LANES)],
            dst_ref=incoming.at[step],
            send_sem=term_send.at[step],
            recv_sem=term_recv.at[step],
            device_id={"chan": target},
            device_id_type=pl.DeviceIdType.MESH,
        )

    @pl.loop(0, count - 1)
    def _(turn):
        term_copy(count - 1 - turn).start()

    mine = lax.div(me * share, LANES)
    incoming[0] = terms[mine]

    @pl.loop(1, count)
    def _(step):
        volt_copy(step).wait_send()
        term_copy(step).wait()

    total = jnp.sum(incoming[...], axis=0)
    geom = geom_all[mine] + column_sum(geom_col[mine])
    updated = gain_ref[:, lane_block(mine)] + 0.5 * total[0:2] / (total[2:3] * geom)
    lane_group = lax.rem(me, LANES // share)
    picked = updated[:, 0:share]
    for group in range(1, LANES // share):
        picked = jnp.where(lane_group == group, updated[:, group * share : (group + 1) * share], picked)
    new_ref[...] = picked


def shards(voltages_real, voltages_imag, model, gains, bandpass):
    count = lax.axis_size("chan")
    samples, channels, inputs = voltages_real.shape
    scale = 1.0 / (4096.0 * samples * count)
    blocks = inputs // LANES
    share = inputs // count
    in_hbm = pl.BlockSpec(memory_space=pltpu.HBM)
    in_vmem = pl.BlockSpec(memory_space=pltpu.VMEM)
    return pl.pallas_call(
        functools.partial(kernel, count, scale),
        out_shape=(
            pltpu.VMEM((1,) + model.shape, F32),
            jax.ShapeDtypeStruct((2, share), F32),
        ),
        in_specs=[in_hbm, in_hbm, in_hbm, in_hbm, pl.BlockSpec(memory_space=pltpu.SMEM)],
        out_specs=(in_vmem, in_vmem),
        scratch_shapes=[
            pltpu.VMEM((2, blocks, samples * channels, LANES), jnp.int32),
            pltpu.VMEM((count, 2 * samples, inputs), BF16),
            pltpu.VMEM((count, 2 * samples, inputs), BF16),
            pltpu.VMEM((count, 2 * samples, inputs), BF16),
            pltpu.VMEM(model.shape, BF16),
            pltpu.VMEM(gains.shape, F32),
            pltpu.VMEM((2, inputs, LANES), F32),
            pltpu.VMEM((2, LANES, LANES), F32),
            pltpu.VMEM((blocks, 2, 8, LANES), F32),
            pltpu.VMEM((blocks, 8, LANES), F32),
            pltpu.VMEM((blocks, 1, LANES), F32),
            pltpu.VMEM((blocks, 8, LANES), F32),
            pltpu.VMEM((count, 8, LANES), F32),
            pltpu.SemaphoreType.DMA((2, blocks)),
            pltpu.SemaphoreType.DMA,
            pltpu.SemaphoreType.DMA,
            pltpu.SemaphoreType.DMA((count,)),
            pltpu.SemaphoreType.DMA((count,)),
            pltpu.SemaphoreType.DMA((count,)),
            pltpu.SemaphoreType.DMA((count,)),
        ],
        compiler_params=pltpu.CompilerParams(
            collective_id=0, has_side_effects=True, vmem_limit_bytes=52 * 1024 * 1024
        ),
        cost_estimate=pl.CostEstimate(
            flops=4 * samples * count * inputs * inputs, bytes_accessed=10 * 1024 * 1024, transcendentals=0
        ),
    )(
        voltages_real.reshape(samples * channels, inputs),
        voltages_imag.reshape(samples * channels, inputs),
        model,
        gains,
        bandpass,
    )


def solution(mesh):
    in_specs = (
        P("chan", "grp", None),
        P("chan", "grp", None),
        P(),
        P(None, "grp"),
        P(("grp", "chan")),
    )
    out_specs = (P(("grp", "chan"), None, None, None), P(None, ("grp", "chan")))
    return jax.shard_map(shards, mesh=mesh, in_specs=in_specs, out_specs=out_specs, check_vma=False)
```

```python
import functools

import jax
import jax.numpy as jnp
from jax import lax
from jax.experimental import pallas as pl
from jax.experimental.pallas import tpu as pltpu
from jax.sharding import PartitionSpec as P

F32 = jnp.float32
BF16 = jnp.bfloat16
LANES = 128


def partner_of(me, step, count):
    total = 0
    bit = 1
    while bit < count:
        total = total + lax.rem(lax.div(me, bit) + lax.div(step, bit), 2) * bit
        bit *= 2
    return total


def lane_block(index):
    return pl.ds(pl.multiple_of(index * LANES, LANES), LANES)


def fold_rows(block):
    return jnp.sum(block.reshape(block.shape[0] // 8, 8, block.shape[1]), axis=0)


def column_sum(block):
    return jnp.sum(block, axis=0, keepdims=True)


def stripe_groups(blocks):
    edges = sorted({0, blocks // 2, 3 * blocks // 4, blocks - 1, blocks})
    return tuple(zip(edges[:-1], edges[1:]))


def kernel(
    count,
    groups,
    scale,
    vr_hbm,
    vi_hbm,
    model_hbm,
    gain_hbm,
    band_ref,
    res_ref,
    new_ref,
    ints,
    outgoing,
    volts,
    swapped,
    model,
    gain_ref,
    gain_rows,
    row_acc,
    col_acc,
    geom_col,
    geom_all,
    terms,
    incoming,
    load_sem,
    model_sem,
    gain_sem,
    send_sem,
    recv_sem,
    term_send,
    term_recv,
):
    me = lax.axis_index("chan")
    inputs = gain_ref.shape[1]
    blocks = inputs // LANES
    samples = ints.shape[2] // count
    share = new_ref.shape[1]

    loads = []
    for which, source in enumerate((vr_hbm, vi_hbm)):
        for lane in range(blocks):
            load = pltpu.make_async_copy(
                source.at[:, lane * LANES : (lane + 1) * LANES],
                ints.at[which, lane],
                load_sem.at[which, lane],
            )
            load.start()
            loads.append(load)
    load_gains = pltpu.make_async_copy(gain_hbm, gain_ref, gain_sem)
    load_model = pltpu.make_async_copy(model_hbm, model, model_sem)

    barrier = pltpu.get_barrier_semaphore()

    @pl.loop(1, count)
    def _(step):
        pl.semaphore_signal(
            barrier,
            inc=1,
            device_id={"chan": partner_of(me, step, count)},
            device_id_type=pl.DeviceIdType.MESH,
        )

    for load in loads:
        load.wait()
    load_gains.start()
    load_model.start()
    pl.semaphore_wait(barrier, count - 1)

    def volt_copy(step, group):
        first, last = groups[group]
        cols = slice(first * LANES, last * LANES)
        return pltpu.make_async_remote_copy(
            src_ref=outgoing.at[step, :, cols],
            dst_ref=volts.at[step, :, cols],
            send_sem=send_sem.at[group, step],
            recv_sem=recv_sem.at[group, step],
            device_id={"chan": partner_of(me, step, count)},
            device_id_type=pl.DeviceIdType.MESH,
        )

    def short_rows(which, channel, lane):
        rows = ints[which, lane, pl.ds(channel, samples, stride=count), :]
        return rows.astype(F32).astype(BF16)

    for group, (first, last) in enumerate(groups):

        @pl.loop(0, count - 1)
        def _(turn):
            step = count - 1 - turn
            channel = partner_of(me, step, count)
            for lane in range(first, last):
                cols = slice(lane * LANES, (lane + 1) * LANES)
                outgoing[step, 0:samples, cols] = short_rows(0, channel, lane)
                outgoing[step, samples : 2 * samples, cols] = short_rows(1, channel, lane)
            volt_copy(step, group).start()

    for lane in range(blocks):
        cols = slice(lane * LANES, (lane + 1) * LANES)
        volts[0, 0:samples, cols] = short_rows(0, me, lane)
        volts[0, samples : 2 * samples, cols] = short_rows(1, me, lane)

    band = band_ref[0]
    load_gains.wait()

    @pl.loop(0, blocks)
    def _(p):
        for part in range(2):
            line = gain_ref[part : part + 1, lane_block(p)]
            gain_rows[part, lane_block(p), :] = jnp.broadcast_to(line, (LANES, LANES)).T
        geom_col[p] = jnp.zeros((8, LANES), F32)
        col_acc[p] = jnp.zeros((2, 8, LANES), F32)

    load_model.wait()

    @pl.loop(0, blocks)
    def _(p):
        row_acc[0] = jnp.zeros((LANES, LANES), F32)
        rows = lane_block(p)

        @pl.loop(0, p + 1)
        def _(j):
            place = lane_block(lax.div(p * (p + 1), 2) + j)
            model_real = model[0, :, place].astype(F32)
            model_imag = model[1, :, place].astype(F32)
            row_real = gain_rows[0, rows, :]
            row_imag = gain_rows[1, rows, :]
            col_real = gain_ref[0:1, lane_block(j)]
            col_imag = gain_ref[1:2, lane_block(j)]
            outer_real = row_real * col_real + row_imag * col_imag
            outer_imag = row_imag * col_real - row_real * col_imag
            res_ref[0, 0, :, place] = -band * (outer_real * model_real - outer_imag * model_imag)
            res_ref[0, 1, :, place] = -band * (outer_real * model_imag + outer_imag * model_real)
            weight_sq = model_real * model_real + model_imag * model_imag
            row_acc[0] += weight_sq * (col_real * col_real + col_imag * col_imag)
            geom_col[j] += fold_rows((row_real * row_real + row_imag * row_imag) * weight_sq)

        geom_all[p] = column_sum(row_acc[0].T)

    def finish_stripes(group):
        first, last = groups[group]
        cols = slice(first * LANES, last * LANES)

        @pl.loop(1, count)
        def _(step):
            volt_copy(step, group).wait_recv()

        @pl.loop(0, count)
        def _(step):
            swapped[step, 0:samples, cols] = -volts[step, samples : 2 * samples, cols]
            swapped[step, samples : 2 * samples, cols] = volts[step, 0:samples, cols]

        depth = 2 * samples * count
        start = first
        while start < last:
            stop = min(start + 2, last)
            span = (stop - start) * LANES
            left = volts[:, :, start * LANES : stop * LANES].reshape(depth, span)
            for tile in range(0, stop, 2):
                end = min(tile + 2, stop)
                for part, source in ((0, volts), (1, swapped)):
                    right = source[:, :, tile * LANES : end * LANES].reshape(depth, (end - tile) * LANES)
                    product = scale * lax.dot_general(
                        left, right, (((0,), (0,)), ((), ())), preferred_element_type=F32
                    )
                    for stripe in range(start, stop):
                        offset = (stripe * (stripe + 1) // 2 + tile) * LANES
                        width = (min(end, stripe + 1) - tile) * LANES
                        top = (stripe - start) * LANES
                        res_ref[0, part, :, offset : offset + width] += product[top : top + LANES, :width]
            start = stop

        pl.loop(first, last)(stripe_terms)

    def stripe_terms(p):
        row_acc[...] = jnp.zeros((2, LANES, LANES), F32)
        rows = lane_block(p)

        @pl.loop(0, p + 1)
        def _(j):
            place = lane_block(lax.div(p * (p + 1), 2) + j)
            model_real = model[0, :, place].astype(F32)
            model_imag = model[1, :, place].astype(F32)
            res_real = res_ref[0, 0, :, place]
            res_imag = res_ref[0, 1, :, place]
            q_real = (band * (res_real * model_real + res_imag * model_imag)).astype(BF16).astype(F32)
            q_imag = (band * (res_imag * model_real - res_real * model_imag)).astype(BF16).astype(F32)
            col_real = gain_ref[0:1, lane_block(j)].astype(BF16).astype(F32)
            col_imag = gain_ref[1:2, lane_block(j)].astype(BF16).astype(F32)
            row_real = gain_rows[0, rows, :].astype(BF16).astype(F32)
            row_imag = gain_rows[1, rows, :].astype(BF16).astype(F32)
            row_acc[0] += q_real * col_real - q_imag * col_imag
            row_acc[1] += q_real * col_imag + q_imag * col_real
            col_acc[j, 0] += fold_rows(row_real * q_real + row_imag * q_imag)
            col_acc[j, 1] += fold_rows(row_imag * q_real - row_real * q_imag)

        terms[p, 0:1] = column_sum(row_acc[0].T)
        terms[p, 1:2] = column_sum(row_acc[1].T)
        terms[p, 2:3] = jnp.full((1, LANES), band * band, F32)
        terms[p, 3:8] = jnp.zeros((5, LANES), F32)

    for group in range(len(groups)):
        finish_stripes(group)

    @pl.loop(0, blocks)
    def _(p):
        terms[p, 0:1] += column_sum(col_acc[p, 0])
        terms[p, 1:2] += column_sum(col_acc[p, 1])

    def term_copy(step):
        target = partner_of(me, step, count)
        return pltpu.make_async_remote_copy(
            src_ref=terms.at[lax.div(target * share, LANES)],
            dst_ref=incoming.at[step],
            send_sem=term_send.at[step],
            recv_sem=term_recv.at[step],
            device_id={"chan": target},
            device_id_type=pl.DeviceIdType.MESH,
        )

    @pl.loop(0, count - 1)
    def _(turn):
        term_copy(count - 1 - turn).start()

    mine = lax.div(me * share, LANES)
    incoming[0] = terms[mine]

    @pl.loop(1, count)
    def _(step):
        for group in range(len(groups)):
            volt_copy(step, group).wait_send()
        term_copy(step).wait()

    total = jnp.sum(incoming[...], axis=0)
    geom = geom_all[mine] + column_sum(geom_col[mine])
    updated = gain_ref[:, lane_block(mine)] + 0.5 * total[0:2] / (total[2:3] * geom)
    lane_group = lax.rem(me, LANES // share)
    picked = updated[:, 0:share]
    for group in range(1, LANES // share):
        picked = jnp.where(lane_group == group, updated[:, group * share : (group + 1) * share], picked)
    new_ref[...] = picked


def shards(voltages_real, voltages_imag, model, gains, bandpass):
    count = lax.axis_size("chan")
    samples, channels, inputs = voltages_real.shape
    scale = 1.0 / (4096.0 * samples * count)
    blocks = inputs // LANES
    share = inputs // count
    groups = stripe_groups(blocks)
    in_hbm = pl.BlockSpec(memory_space=pltpu.HBM)
    in_vmem = pl.BlockSpec(memory_space=pltpu.VMEM)
    return pl.pallas_call(
        functools.partial(kernel, count, groups, scale),
        out_shape=(
            pltpu.VMEM((1,) + model.shape, F32),
            jax.ShapeDtypeStruct((2, share), F32),
        ),
        in_specs=[in_hbm, in_hbm, in_hbm, in_hbm, pl.BlockSpec(memory_space=pltpu.SMEM)],
        out_specs=(in_vmem, in_vmem),
        scratch_shapes=[
            pltpu.VMEM((2, blocks, samples * channels, LANES), jnp.int32),
            pltpu.VMEM((count, 2 * samples, inputs), BF16),
            pltpu.VMEM((count, 2 * samples, inputs), BF16),
            pltpu.VMEM((count, 2 * samples, inputs), BF16),
            pltpu.VMEM(model.shape, BF16),
            pltpu.VMEM(gains.shape, F32),
            pltpu.VMEM((2, inputs, LANES), F32),
            pltpu.VMEM((2, LANES, LANES), F32),
            pltpu.VMEM((blocks, 2, 8, LANES), F32),
            pltpu.VMEM((blocks, 8, LANES), F32),
            pltpu.VMEM((blocks, 1, LANES), F32),
            pltpu.VMEM((blocks, 8, LANES), F32),
            pltpu.VMEM((count, 8, LANES), F32),
            pltpu.SemaphoreType.DMA((2, blocks)),
            pltpu.SemaphoreType.DMA,
            pltpu.SemaphoreType.DMA,
            pltpu.SemaphoreType.DMA((len(groups), count)),
            pltpu.SemaphoreType.DMA((len(groups), count)),
            pltpu.SemaphoreType.DMA((count,)),
            pltpu.SemaphoreType.DMA((count,)),
        ],
        compiler_params=pltpu.CompilerParams(
            collective_id=0, has_side_effects=True, vmem_limit_bytes=52 * 1024 * 1024
        ),
        cost_estimate=pl.CostEstimate(
            flops=4 * samples * count * inputs * inputs, bytes_accessed=10 * 1024 * 1024, transcendentals=0
        ),
    )(
        voltages_real.reshape(samples * channels, inputs),
        voltages_imag.reshape(samples * channels, inputs),
        model,
        gains,
        bandpass,
    )


def solution(mesh):
    in_specs = (
        P("chan", "grp", None),
        P("chan", "grp", None),
        P(),
        P(None, "grp"),
        P(("grp", "chan")),
    )
    out_specs = (P(("grp", "chan"), None, None, None), P(None, ("grp", "chan")))
    return jax.shard_map(shards, mesh=mesh, in_specs=in_specs, out_specs=out_specs, check_vma=False)
```
